256 devices in a mesh: pts: 32 (over y, x, z_lo), modes: 8 (over z_hi, core).
Axes of the slice: x: 4, y: 4, z: 8 (z_hi: 4, z_lo: 2; z = z_hi * 2 + z_lo), core: 2. Of those that a mesh axis runs over, the one named last changes fastest.
Arguments:
- mode_stress: bfloat16 [6, 4096, 2048], P(None, 'pts', 'modes'), may hold values from -0.125 to 0.125
- histories: bfloat16 [16384, 2048], P(('pts', 'modes')), may hold values from -6 to 6
Outputs:
- peak_mises: float32 [4096], P('pts')
- root_mean: float32 [4096], P('pts')
The draws below stay inside these ranges and needn't reach their ends.
All inputs are finite; a program needn't handle non-finite values.
Results may differ from the reference program's by a relative error of at most 0.0003.
Values may be sent and summed in bfloat16 or wider, within the bound.
A program may use at most 128 MiB of HBM per device.

```python
import jax
import jax.numpy as jnp
from jax import lax

MODES = 2048
COMPS = 6
STEPS = 16384
PT_DEV = 128
POINTS = 4096


def steps_of(own_key, dims, split, low, high):
    def one(dim, shards_of):
        steps = jax.random.uniform(jax.random.fold_in(jax.random.fold_in(own_key, 6), dim), (shards_of,), jnp.float32, low / len(split), high / len(split))
        return jnp.repeat(jnp.exp(steps), dims[dim] // shards_of).reshape((-1,) + (1,) * (len(dims) - dim - 1))

    gain = one(*split[0])
    for cut in split[1:]:
        gain = gain * one(*cut)
    return gain


def centred(stream_key, dims, deviation, limit, split=(), held_as=jnp.bfloat16):
    entries = jax.random.normal(stream_key, dims, jnp.float32) * deviation
    if len(split) > 0:
        entries = steps_of(stream_key, dims, split, -0.22, 0.18) * entries
    return jnp.clip(entries, min=-limit, max=limit).astype(held_as)


def setup_inputs(seed: int = 0) -> dict:
    arg_keys = jax.random.split(jax.random.key(seed), 3)
    return {
        "mode_stress": centred(arg_keys[0], (COMPS, POINTS, MODES), MODES ** -0.5, 0.125, ((1, 32), (2, 8))),
        "histories": centred(arg_keys[1], (STEPS, MODES), 1.0, 6.0, ((0, 256),)),
    }


def squared_mises(stress):
    sxx, syy, szz = (stress[0], stress[1], stress[2])
    normal = (sxx - syy) ** 2 + (syy - szz) ** 2 + (szz - sxx) ** 2
    shear = stress[3] ** 2 + stress[4] ** 2 + stress[5] ** 2
    return 0.5 * normal + 3.0 * shear

def reference(mode_stress, histories):
    coords = histories.astype(jnp.float32)
    blocks = mode_stress.reshape(COMPS, POINTS // PT_DEV, PT_DEV, MODES).transpose(1, 0, 2, 3)

    def one_block(block):
        stress = jnp.einsum('cpm,tm->cpt', block.astype(jnp.float32), coords, precision=lax.Precision.HIGHEST)
        squared = squared_mises(stress)
        return (lax.optimization_barrier(jnp.max(squared, axis=1)), lax.optimization_barrier(jnp.sum(squared, axis=1)))
    highest, summed = lax.map(one_block, blocks)
    highest = highest.reshape(POINTS)
    summed = summed.reshape(POINTS)
    return (jnp.sqrt(highest), jnp.sqrt(summed / STEPS + 1e-06))
```

```python
import jax
import jax.numpy as jnp
from jax import lax
from jax.experimental import pallas as pl
from jax.experimental.pallas import tpu as pltpu
from jax.sharding import PartitionSpec as P

STEPS = 16384
MESH = pl.DeviceIdType.MESH
SIDE = 4
DEPTH = 8
PARTS = 6
POINTS = 128
HALF = 128
ROWS = 32
QUARTER = 16
PLACE = (0, 1, 3, 2)


def kernel(stress_ref, hist_ref, out_ref, sbuf, hbuf, acc, part, inbox, load_sem, send_sem, recv_sem):
    pts, modes = lax.axis_index("pts"), lax.axis_index("modes")
    x, y = lax.rem(pts // 2, SIDE), pts // (2 * SIDE)
    z, core = (modes // 2) * 2 + lax.rem(pts, 2), lax.rem(modes, 2)

    def device(dx=0, dy=0, dz=0, dc=0):
        px, py = lax.rem(x + dx + SIDE, SIDE), lax.rem(y + dy + SIDE, SIDE)
        pz = lax.rem(z + dz + DEPTH, DEPTH)
        pc = 1 - core if dc else core
        return ((py * SIDE + px) * 2 + lax.rem(pz, 2), (pz // 2) * 2 + pc)

    def along(axis, d):
        return device(dx=d) if axis == 0 else device(dy=d)

    copies = {}

    def remote(key, src, dst, target):
        i = len(copies)
        copies[key] = pltpu.make_async_remote_copy(
            src_ref=src, dst_ref=dst, send_sem=send_sem.at[i], recv_sem=recv_sem.at[i],
            device_id=target, device_id_type=MESH,
        )

    for sign in (1, -1):
        for step in range(4):
            source, target = (-sign * step) % DEPTH, (-sign * (step + 1)) % DEPTH
            for half in (0, 1):
                if step == 3 and half != (0 if sign == 1 else 1):
                    continue
                remote(("z", target, half), sbuf.at[source, half, 0], sbuf.at[target, half, 0], device(dz=sign))
    for s in range(DEPTH):
        for half in (0, 1):
            remote(("core", s, half), sbuf.at[s, half, 0], sbuf.at[s, half, 1], device(dc=1))

    def rows(h, second, first, cut):
        block = hbuf.at[PLACE[second], h, first]
        return block if cut is None else block.at[pl.ds(cut * QUARTER, QUARTER)]

    for h in (0, 1):
        for sign in (1, -1):
            near, cut = (-sign) % SIDE, 0 if sign == 1 else 1
            remote(("first", h, near, None), rows(h, 0, 0, None), rows(h, 0, near, None), along(h, sign))
            remote(("first", h, 2, cut), rows(h, 0, near, cut), rows(h, 0, 2, cut), along(h, sign))
            for f in range(SIDE):
                remote(("second", h, f, near, None), rows(h, 0, f, None), rows(h, near, f, None), along(1 - h, sign))
                remote(("second", h, f, 2, cut), rows(h, near, f, cut), rows(h, 2, f, cut), along(1 - h, sign))

    others = [(dz, dc) for dz in range(DEPTH) for dc in (0, 1) if (dz, dc) != (0, 0)]
    for i, (dz, dc) in enumerate(others):
        remote(("part", i), part.at[dz % 2], inbox.at[i], device(dz=dz, dc=dc))

    def start(*keys):
        for key in keys:
            copies[key].start()

    def arrived(*keys):
        for key in keys:
            copies[key].wait_recv()

    seen = set()

    def product(place, count, s):
        base = (lax.rem(z + s, DEPTH) // 2) * (4 * HALF)
        own = pl.multiple_of(base + core * (2 * HALF), 2 * HALF)
        sibling = pl.multiple_of(base + (1 - core) * (2 * HALF), 2 * HALF)
        n = count * 2 * SIDE * ROWS
        left = jnp.concatenate(
            [hbuf[place : place + count, :, :, :, pl.ds(at, 2 * HALF)].reshape(n, 2 * HALF) for at in (own, sibling)],
            axis=1,
        )
        right = jnp.concatenate(
            [sbuf[s, half, c].reshape(PARTS * POINTS, HALF) for c in (0, 1) for half in (0, 1)], axis=1
        )
        return lax.dot_general(left, right, (((1,), (1,)), ((), ())), preferred_element_type=jnp.float32)

    def work(places, slots):
        for place in places:
            for s in slots:
                at = pl.ds(place * 2 * SIDE * ROWS, 2 * SIDE * ROWS)
                value = product(place, 1, s)
                if (s % 2, place) in seen:
                    acc[s % 2, at] += value
                else:
                    acc[s % 2, at] = value
                    seen.add((s % 2, place))

    def squared(value):
        s = [value[:, i * POINTS : (i + 1) * POINTS] for i in range(PARTS)]
        xy, yz, zx = s[0] - s[1], s[1] - s[2], s[2] - s[0]
        return 0.5 * (xy * xy + yz * yz + zx * zx) + 3.0 * (s[3] * s[3] + s[4] * s[4] + s[5] * s[5])

    def reduce(which, last=None):
        highest = jnp.zeros((8, POINTS), jnp.float32)
        summed = jnp.zeros((8, POINTS), jnp.float32)
        n = 2 * SIDE * ROWS
        for place in range(4):
            value = acc[which, pl.ds(place * n, n)]
            if last is not None:
                value = value + product(place, 1, last)
            square = squared(value).reshape(n // 8, 8, POINTS)
            highest = jnp.maximum(highest, jnp.max(square, axis=0))
            summed = summed + jnp.sum(square, axis=0)
        part[which, 0] = highest
        part[which, 1] = summed

    barrier = pltpu.get_barrier_semaphore()
    greeted = [device(dz=dz, dc=dc) for dz, dc in others]
    greeted += [along(axis, sign) for axis in (0, 1) for sign in (1, -1)]
    for other in greeted:
        pl.semaphore_signal(barrier, inc=1, device_id=other, device_id_type=MESH)
    loads = [
        pltpu.make_async_copy(stress_ref.at[:, :, pl.ds(half * HALF, HALF)], sbuf.at[0, half, 0], load_sem.at[half])
        for half in (0, 1)
    ] + [
        pltpu.make_async_copy(hist_ref.at[pl.ds(h * ROWS, ROWS)], hbuf.at[0, h, 0], load_sem.at[2 + h])
        for h in (0, 1)
    ]
    for load in loads:
        load.start()
    for load in loads:
        load.wait()
    pl.semaphore_wait(barrier, len(greeted))

    def ring(step):
        return [(("z", 8 - step, 0), ("z", step, 1)), (("z", 8 - step, 1), ("z", step, 0))]

    def forward(step, turn):
        for _, s, half in ring(step)[turn]:
            arrived(("z", s, half))
            onward = s + 1 if s <= 4 else s - 1
            if ("z", onward, half) in copies and (onward != 4 or (half == 0) == (s > 4)):
                start(("z", onward, half))
            start(("core", s, half))

    def have(s):
        arrived(("core", s, 0), ("core", s, 1))

    start(*ring(1)[0])
    start(*[("first", h, near, None) for near in (3, 1) for h in (0, 1)])
    start(*[("second", h, 0, near, None) for near in (3, 1) for h in (0, 1)])
    start(*ring(1)[1], ("core", 0, 0), ("core", 0, 1))

    cut_of = {3: 0, 1: 1}
    for h in (0, 1):
        for near in (3, 1):
            arrived(("first", h, near, None))
            start(("first", h, 2, cut_of[near]))
    for f in (3, 1):
        for h in (0, 1):
            start(*[("second", h, f, near, None) for near in (3, 1)])
    forward(1, 0)
    for h in (0, 1):
        arrived(("first", h, 2, 0), ("first", h, 2, 1))
        start(*[("second", h, 2, near, None) for near in (3, 1)])

    def fold(f):
        for h in (0, 1):
            for near in (3, 1):
                arrived(("second", h, f, near, None))
                start(("second", h, f, 2, cut_of[near]))

    fold(0)
    forward(1, 1)
    have(0)
    work([0], [0])
    have(1)
    have(7)
    fold(3)
    forward(2, 0)
    work([0], [1, 7])
    fold(1)
    fold(2)
    forward(2, 1)
    work([1, 2], [0, 1, 7])
    forward(3, 0)
    have(2)
    have(6)
    work([0, 1, 2], [2, 6])
    for h in (0, 1):
        for f in range(SIDE):
            arrived(("second", h, f, 2, 0), ("second", h, f, 2, 1))
    work([3], [0, 1, 7, 2, 6])
    forward(3, 1)
    have(3)
    have(5)
    work([0, 1, 2, 3], [3, 5])
    reduce(1)
    for half in (0, 1):
        arrived(("z", 4, half))
        start(("core", 4, half))
    have(4)
    reduce(0, 4)

    parts = [("part", i) for i in range(len(others))]
    start(*parts)
    highest, summed = part[0, 0], part[0, 1]
    for i, key in enumerate(parts):
        arrived(key)
        highest = jnp.maximum(highest, inbox[i, 0])
        summed = summed + inbox[i, 1]
    out_ref[0:1] = jnp.max(highest, axis=0, keepdims=True)
    out_ref[1:2] = jnp.sum(summed, axis=0, keepdims=True)
    for copy in copies.values():
        copy.wait_send()


def on_device(mode_stress, histories):
    n_copies = 14 + 16 + 40 + 15
    out = pl.pallas_call(
        kernel,
        out_shape=jax.ShapeDtypeStruct((2, POINTS), jnp.float32),
        in_specs=[pl.BlockSpec(memory_space=pl.ANY)] * 2,
        out_specs=pl.BlockSpec(memory_space=pltpu.VMEM),
        scratch_shapes=[
            pltpu.VMEM((DEPTH, 2, 2, PARTS, POINTS, HALF), jnp.bfloat16),
            pltpu.VMEM((SIDE, 2, SIDE, ROWS, 2048), jnp.bfloat16),
            pltpu.VMEM((2, 2 * SIDE * SIDE * ROWS, PARTS * POINTS), jnp.float32),
            pltpu.VMEM((2, 2, 8, POINTS), jnp.float32),
            pltpu.VMEM((15, 2, 8, POINTS), jnp.float32),
            pltpu.SemaphoreType.DMA((4,)),
            pltpu.SemaphoreType.DMA((n_copies,)),
            pltpu.SemaphoreType.DMA((n_copies,)),
        ],
        compiler_params=pltpu.CompilerParams(
            collective_id=0, has_side_effects=True, vmem_limit_bytes=48 * 2**20
        ),
        cost_estimate=pl.CostEstimate(
            flops=2 * 1024 * 2048 * 2 * PARTS * POINTS, bytes_accessed=2**20, transcendentals=0
        ),
    )(mode_stress, histories)
    return jnp.sqrt(out[0]), jnp.sqrt(out[1] / STEPS + 1e-06)


def solution(mesh):
    placed = (P(None, "pts", "modes"), P(("pts", "modes"), None))
    return jax.shard_map(
        on_device, mesh=mesh, in_specs=placed, out_specs=(P("pts"), P("pts")), check_vma=False
    )
```

```python
import jax
import jax.numpy as jnp
from jax import lax
from jax.experimental import pallas as pl
from jax.experimental.pallas import tpu as pltpu
from jax.sharding import PartitionSpec as P

STEPS = 16384
MESH = pl.DeviceIdType.MESH
SIDE = 4
DEPTH = 8
PARTS = 6
POINTS = 128
SHARE = 256
ROWS = 32
QUARTER = 16
GROUP = 2 * SIDE * ROWS
PLACE = (0, 1, 3, 2)


def kernel(stress_ref, hist_ref, out_ref, sbuf, hbuf, acc, part, inbox, load_sem, send_sem, recv_sem):
    pts, modes = lax.axis_index("pts"), lax.axis_index("modes")
    x, y = lax.rem(pts // 2, SIDE), pts // (2 * SIDE)
    z, core = (modes // 2) * 2 + lax.rem(pts, 2), lax.rem(modes, 2)

    def device(dx=0, dy=0, dz=0, dc=0):
        px, py = lax.rem(x + dx + SIDE, SIDE), lax.rem(y + dy + SIDE, SIDE)
        pz = lax.rem(z + dz + DEPTH, DEPTH)
        pc = 1 - core if dc else core
        return ((py * SIDE + px) * 2 + lax.rem(pz, 2), (pz // 2) * 2 + pc)

    def along(axis, d):
        return device(dx=d) if axis == 0 else device(dy=d)

    copies = {}

    def remote(key, src, dst, target):
        i = len(copies)
        copies[key] = pltpu.make_async_remote_copy(
            src_ref=src, dst_ref=dst, send_sem=send_sem.at[i], recv_sem=recv_sem.at[i],
            device_id=target, device_id_type=MESH,
        )

    def piece(s, c, low, n):
        return sbuf.at[s, c, pl.ds(low, n)]

    cuts = {s: ((0, 3), (3, 3)) for s in range(DEPTH)}
    cuts[0] = ((0, 6),)
    cuts[4] = tuple((i, 1) for i in range(PARTS))
    for sign in (1, -1):
        for step in range(4):
            source, target = (-sign * step) % DEPTH, (-sign * (step + 1)) % DEPTH
            for low, n in cuts[target]:
                if step == 3 and (low < 3) != (sign == 1):
                    continue
                remote(("z", target, low), piece(source, 0, low, n), piece(target, 0, low, n), device(dz=sign))
    for s in range(DEPTH):
        for low, n in cuts[s]:
            remote(("core", s, low), piece(s, 0, low, n), piece(s, 1, low, n), device(dc=1))

    def rows(h, second, first, cut):
        block = hbuf.at[PLACE[second], h, first]
        return block if cut is None else block.at[pl.ds(cut * QUARTER, QUARTER)]

    for h in (0, 1):
        for sign in (1, -1):
            near, cut = (-sign) % SIDE, 0 if sign == 1 else 1
            remote(("first", h, near, None), rows(h, 0, 0, None), rows(h, 0, near, None), along(h, sign))
            remote(("first", h, 2, cut), rows(h, 0, near, cut), rows(h, 0, 2, cut), along(h, sign))
            for f in range(SIDE):
                remote(("second", h, f, near, None), rows(h, 0, f, None), rows(h, near, f, None), along(1 - h, sign))
                remote(("second", h, f, 2, cut), rows(h, near, f, cut), rows(h, 2, f, cut), along(1 - h, sign))

    others = [(dz, dc) for dz in (4, 3, 5, 2, 6, 1, 7, 0) for dc in (0, 1) if (dz, dc) != (0, 0)]
    for i, (dz, dc) in enumerate(others):
        remote(("part", i), part.at[dz % 2], inbox.at[i], device(dz=dz, dc=dc))

    def start(*keys):
        for key in keys:
            copies[key].start()

    def arrived(*keys):
        for key in keys:
            copies[key].wait_recv()

    seen = set()

    def product(place, count, s, parts, shares=(0, 1)):
        base = (lax.rem(z + s, DEPTH) // 2) * (2 * SHARE)
        left, right = [], []
        for c in shares:
            first = pl.multiple_of(base + (1 - core if c else core) * SHARE, SHARE)
            left.append(hbuf[place : place + count, :, :, :, pl.ds(first, SHARE)].reshape(count * GROUP, SHARE))
            right.append(jnp.concatenate([sbuf[s, c, i] for i in parts], axis=0))
        left, right = (v[0] if len(v) == 1 else jnp.concatenate(v, axis=1) for v in (left, right))
        return lax.dot_general(left, right, (((1,), (1,)), ((), ())), preferred_element_type=jnp.float32)

    def work(place, count, slots, parts=tuple(range(PARTS)), shares=(0, 1)):
        at = pl.ds(place * GROUP, count * GROUP)
        for s in slots:
            value = product(place, count, s, parts, shares)
            for k, i in enumerate(parts):
                lanes, term = pl.ds(i * POINTS, POINTS), value[:, k * POINTS : (k + 1) * POINTS]
                blocks = {(s % 2, p, i) for p in range(place, place + count)}
                assert blocks <= seen or not blocks & seen
                if blocks <= seen:
                    acc[s % 2, at, lanes] += term
                else:
                    acc[s % 2, at, lanes] = term
                seen.update(blocks)

    def squared(s):
        xy, yz, zx = s[0] - s[1], s[1] - s[2], s[2] - s[0]
        return 0.5 * (xy * xy + yz * yz + zx * zx) + 3.0 * (s[3] * s[3] + s[4] * s[4] + s[5] * s[5])

    def reduce(which, last=()):
        highest = jnp.zeros((8, POINTS), jnp.float32)
        summed = jnp.zeros((8, POINTS), jnp.float32)
        for place in range(4):
            value = [acc[which, pl.ds(place * GROUP, GROUP), pl.ds(i * POINTS, POINTS)] for i in range(PARTS)]
            if last:
                rest = product(place, 1, 4, last, (1,))
                for k, i in enumerate(last):
                    value[i] = value[i] + rest[:, k * POINTS : (k + 1) * POINTS]
            square = squared(value).reshape(GROUP // 8, 8, POINTS)
            highest = jnp.maximum(highest, jnp.max(square, axis=0))
            summed = summed + jnp.sum(square, axis=0)
        part[which, 0:1] = jnp.max(highest, axis=0, keepdims=True)
        part[which, 1:2] = jnp.sum(summed, axis=0, keepdims=True)

    loads = [
        pltpu.make_async_copy(stress_ref.at[pl.ds(low, 3)], piece(0, 0, low, 3), load_sem.at[i])
        for i, low in enumerate((0, 3))
    ] + [
        pltpu.make_async_copy(hist_ref.at[pl.ds(h * ROWS, ROWS)], hbuf.at[0, h, 0], load_sem.at[2 + h])
        for h in (0, 1)
    ]
    for load in loads:
        load.start()
    barrier = pltpu.get_barrier_semaphore()
    greeted = [device(dz=1), device(dz=-1), device(dc=1)]
    greeted += [along(axis, sign) for axis in (0, 1) for sign in (1, -1)]
    for other in greeted:
        pl.semaphore_signal(barrier, inc=1, device_id=other, device_id_type=MESH)
    for load in loads:
        load.wait()
    pl.semaphore_wait(barrier, len(greeted))

    def ring(step):
        return [((8 - step, 0), (step, 3)), ((8 - step, 3), (step, 0))]

    def forward(step, turn):
        for s, low in ring(step)[turn]:
            arrived(("z", s, low))
            if step < 3:
                start(("z", s + 1 if s < 4 else s - 1, low))
            elif turn == 0:
                start(*[("z", 4, low + i) for i in range(3)])
        start(*[("core", s, low) for s, low in ring(step)[turn]])

    def have(s):
        arrived(*[("core", s, low) for low, _ in cuts[s]])

    start(("z", 7, 0), ("z", 1, 3))
    start(*[("first", h, near, None) for near in (3, 1) for h in (0, 1)])
    start(("z", 7, 3), ("z", 1, 0))
    start(*[("second", h, 0, near, None) for near in (3, 1) for h in (0, 1)])
    start(("core", 0, 0))

    cut_of = {3: 0, 1: 1}
    for h in (0, 1):
        for near in (3, 1):
            arrived(("first", h, near, None))
            start(("first", h, 2, cut_of[near]))
    for f in (3, 1):
        for h in (0, 1):
            start(*[("second", h, f, near, None) for near in (3, 1)])
    forward(1, 0)
    for h in (0, 1):
        arrived(("first", h, 2, 0), ("first", h, 2, 1))
        start(*[("second", h, 2, near, None) for near in (3, 1)])

    def fold(f):
        for h in (0, 1):
            for near in (3, 1):
                arrived(("second", h, f, near, None))
                start(("second", h, f, 2, cut_of[near]))

    fold(0)
    forward(1, 1)
    have(0)
    work(0, 1, [0])
    have(1)
    have(7)
    fold(3)
    forward(2, 0)
    work(0, 1, [1, 7])
    fold(1)
    forward(2, 1)
    fold(2)
    work(1, 2, [0, 1, 7])
    have(2)
    have(6)
    work(0, 3, [2, 6])
    forward(3, 0)
    for h in (0, 1):
        for f in range(SIDE):
            arrived(("second", h, f, 2, 0), ("second", h, f, 2, 1))
    work(3, 1, [0, 1, 7, 2, 6])
    arrived(("core", 5, 0), ("core", 3, 3))
    work(0, 4, [5], (0, 1, 2))
    work(0, 4, [3], (3, 4, 5))
    forward(3, 1)
    arrived(("core", 5, 3), ("core", 3, 0))
    work(0, 4, [5], (3, 4, 5))
    work(0, 4, [3], (0, 1, 2))
    for i in range(3):
        for low in (i, 3 + i):
            arrived(("z", 4, low))
            start(("core", 4, low))
        if i:
            arrived(("core", 4, i - 1), ("core", 4, i + 2))
            work(0, 4, [4], (i - 1, i + 2), (1,))
        work(0, 4, [4], (i, 3 + i), (0,))
    reduce(1)
    start(*[("part", i) for i, (dz, _) in enumerate(others) if dz % 2])
    arrived(("core", 4, 2), ("core", 4, 5))
    reduce(0, (2, 5))

    start(*[("part", i) for i, (dz, _) in enumerate(others) if dz % 2 == 0])
    arrived(*[("part", i) for i in range(len(others))])
    out_ref[0:1] = jnp.max(
        jnp.concatenate([part[0, 0:1]] + [inbox[i, 0:1] for i in range(len(others))]), axis=0, keepdims=True
    )
    out_ref[1:2] = jnp.sum(
        jnp.concatenate([part[0, 1:2]] + [inbox[i, 1:2] for i in range(len(others))]), axis=0, keepdims=True
    )
    for copy in copies.values():
        copy.wait_send()


def on_device(mode_stress, histories):
    n_copies = 18 + 19 + 40 + 15
    out = pl.pallas_call(
        kernel,
        out_shape=jax.ShapeDtypeStruct((2, POINTS), jnp.float32),
        in_specs=[pl.BlockSpec(memory_space=pl.ANY)] * 2,
        out_specs=pl.BlockSpec(memory_space=pltpu.VMEM),
        scratch_shapes=[
            pltpu.VMEM((DEPTH, 2, PARTS, POINTS, SHARE), jnp.bfloat16),
            pltpu.VMEM((SIDE, 2, SIDE, ROWS, 2048), jnp.bfloat16),
            pltpu.VMEM((2, 4 * GROUP, PARTS * POINTS), jnp.float32),
            pltpu.VMEM((2, 2, POINTS), jnp.float32),
            pltpu.VMEM((15, 2, POINTS), jnp.float32),
            pltpu.SemaphoreType.DMA((4,)),
            pltpu.SemaphoreType.DMA((n_copies,)),
            pltpu.SemaphoreType.DMA((n_copies,)),
        ],
        compiler_params=pltpu.CompilerParams(
            collective_id=0, has_side_effects=True, vmem_limit_bytes=(53 * 1024 + 816) * 1024
        ),
        cost_estimate=pl.CostEstimate(
            flops=2 * 1024 * 2048 * 2 * PARTS * POINTS, bytes_accessed=2**20, transcendentals=0
        ),
    )(mode_stress, histories)
    return jnp.sqrt(out[0]), jnp.sqrt(out[1] / STEPS + 1e-06)


def solution(mesh):
    placed = (P(None, "pts", "modes"), P(("pts", "modes"), None))
    return jax.shard_map(
        on_device, mesh=mesh, in_specs=placed, out_specs=(P("pts"), P("pts")), check_vma=False
    )
```

```python
import jax
import jax.numpy as jnp
from jax import lax
from jax.experimental import pallas as pl
from jax.experimental.pallas import tpu as pltpu
from jax.sharding import PartitionSpec as P

STEPS = 16384
MESH = pl.DeviceIdType.MESH
SIDE = 4
DEPTH = 8
PARTS = 6
POINTS = 128
SHARE = 256
ROWS = 32
QUARTER = 16
GROUP = 2 * SIDE * ROWS
PLACE = (0, 1, 3, 2)


def kernel(stress_ref, hist_ref, out_ref, sbuf, hbuf, acc, part, inbox, load_sem, send_sem, recv_sem):
    pts, modes = lax.axis_index("pts"), lax.axis_index("modes")
    x, y = lax.rem(pts // 2, SIDE), pts // (2 * SIDE)
    z, core = (modes // 2) * 2 + lax.rem(pts, 2), lax.rem(modes, 2)

    def device(dx=0, dy=0, dz=0, dc=0):
        px, py = lax.rem(x + dx + SIDE, SIDE), lax.rem(y + dy + SIDE, SIDE)
        pz = lax.rem(z + dz + DEPTH, DEPTH)
        pc = 1 - core if dc else core
        return ((py * SIDE + px) * 2 + lax.rem(pz, 2), (pz // 2) * 2 + pc)

    def along(axis, d):
        return device(dx=d) if axis == 0 else device(dy=d)

    copies = {}

    def remote(key, src, dst, target):
        i = len(copies)
        copies[key] = pltpu.make_async_remote_copy(
            src_ref=src, dst_ref=dst, send_sem=send_sem.at[i], recv_sem=recv_sem.at[i],
            device_id=target, device_id_type=MESH,
        )

    def piece(s, c, low, n):
        return sbuf.at[s, c, pl.ds(low, n)]

    cuts = {s: ((0, 3), (3, 3)) for s in range(DEPTH)}
    cuts[0] = ((0, 6),)
    cuts[3] = cuts[5] = ((0, 2), (2, 2), (4, 2))
    cuts[4] = ((0, 2), (2, 1), (3, 1), (4, 2))
    for sign in (1, -1):
        for step in range(4):
            source, target = (-sign * step) % DEPTH, (-sign * (step + 1)) % DEPTH
            for low, n in cuts[target]:
                if step == 3 and (low < 3) != (sign == 1):
                    continue
                remote(("z", target, low), piece(source, 0, low, n), piece(target, 0, low, n), device(dz=sign))
    for s in range(DEPTH):
        for low, n in cuts[s]:
            remote(("core", s, low), piece(s, 0, low, n), piece(s, 1, low, n), device(dc=1))

    def rows(h, second, first, cut):
        block = hbuf.at[PLACE[second], h, first]
        return block if cut is None else block.at[pl.ds(cut * QUARTER, QUARTER)]

    for h in (0, 1):
        for sign in (1, -1):
            near, cut = (-sign) % SIDE, 0 if sign == 1 else 1
            remote(("first", h, near, None), rows(h, 0, 0, None), rows(h, 0, near, None), along(h, sign))
            remote(("first", h, 2, cut), rows(h, 0, near, cut), rows(h, 0, 2, cut), along(h, sign))
            for f in range(SIDE):
                remote(("second", h, f, near, None), rows(h, 0, f, None), rows(h, near, f, None), along(1 - h, sign))
                remote(("second", h, f, 2, cut), rows(h, near, f, cut), rows(h, 2, f, cut), along(1 - h, sign))

    others = [(dz, dc) for dz in (4, 3, 5, 2, 6, 1, 7, 0) for dc in (0, 1) if (dz, dc) != (0, 0)]
    for i, (dz, dc) in enumerate(others):
        remote(("part", i), part.at[dz % 2], inbox.at[i], device(dz=dz, dc=dc))

    def start(*keys):
        for key in keys:
            copies[key].start()

    def arrived(*keys):
        for key in keys:
            copies[key].wait_recv()

    seen = set()

    def product(place, count, s, parts, shares=(0, 1)):
        base = (lax.rem(z + s, DEPTH) // 2) * (2 * SHARE)
        left, right = [], []
        for c in shares:
            first = pl.multiple_of(base + (1 - core if c else core) * SHARE, SHARE)
            left.append(hbuf[place : place + count, :, :, :, pl.ds(first, SHARE)].reshape(count * GROUP, SHARE))
            right.append(jnp.concatenate([sbuf[s, c, i] for i in parts], axis=0))
        left, right = (v[0] if len(v) == 1 else jnp.concatenate(v, axis=1) for v in (left, right))
        return lax.dot_general(left, right, (((1,), (1,)), ((), ())), preferred_element_type=jnp.float32)

    def work(place, count, slots, parts=tuple(range(PARTS)), shares=(0, 1)):
        at = pl.ds(place * GROUP, count * GROUP)
        for s in slots:
            value = product(place, count, s, parts, shares)
            for k, i in enumerate(parts):
                lanes, term = pl.ds(i * POINTS, POINTS), value[:, k * POINTS : (k + 1) * POINTS]
                blocks = {(s % 2, p, i) for p in range(place, place + count)}
                assert blocks <= seen or not blocks & seen
                if blocks <= seen:
                    acc[s % 2, at, lanes] += term
                else:
                    acc[s % 2, at, lanes] = term
                seen.update(blocks)

    def squared(s):
        xy, yz, zx = s[0] - s[1], s[1] - s[2], s[2] - s[0]
        return 0.5 * (xy * xy + yz * yz + zx * zx) + 3.0 * (s[3] * s[3] + s[4] * s[4] + s[5] * s[5])

    def reduce(which, last=()):
        highest = jnp.zeros((8, POINTS), jnp.float32)
        summed = jnp.zeros((8, POINTS), jnp.float32)
        for place in range(4):
            value = [acc[which, pl.ds(place * GROUP, GROUP), pl.ds(i * POINTS, POINTS)] for i in range(PARTS)]
            if last:
                rest = product(place, 1, 4, last, (1,))
                for k, i in enumerate(last):
                    value[i] = value[i] + rest[:, k * POINTS : (k + 1) * POINTS]
            square = squared(value).reshape(GROUP // 8, 8, POINTS)
            highest = jnp.maximum(highest, jnp.max(square, axis=0))
            summed = summed + jnp.sum(square, axis=0)
        part[which, 0:1] = jnp.max(highest, axis=0, keepdims=True)
        part[which, 1:2] = jnp.sum(summed, axis=0, keepdims=True)

    barrier = pltpu.get_barrier_semaphore()
    greeted = [device(dz=1), device(dz=-1)] + [along(axis, sign) for axis in (0, 1) for sign in (1, -1)]
    greeted += [device(dc=1)]
    for other in greeted:
        pl.semaphore_signal(barrier, inc=1, device_id=other, device_id_type=MESH)
    loads = [
        pltpu.make_async_copy(stress_ref.at[pl.ds(low, 3)], piece(0, 0, low, 3), load_sem.at[i])
        for i, low in enumerate((0, 3))
    ] + [
        pltpu.make_async_copy(hist_ref.at[pl.ds(h * ROWS, ROWS)], hbuf.at[0, h, 0], load_sem.at[2 + h])
        for h in (0, 1)
    ]
    for load in loads:
        load.start()
    pl.semaphore_wait(barrier, len(greeted))

    def forward(*moves):
        for s, low, onward in moves:
            arrived(("z", s, low))
            start(*onward)
        start(*[("core", s, low) for s, low, _ in moves])

    def have(s):
        arrived(*[("core", s, low) for low, _ in cuts[s]])

    loads[0].wait()
    loads[1].wait()
    start(("z", 7, 0), ("z", 1, 3))
    loads[2].wait()
    loads[3].wait()
    start(*[("first", h, near, None) for near in (3, 1) for h in (0, 1)])
    start(("z", 7, 3), ("z", 1, 0))
    start(*[("second", h, 0, near, None) for near in (3, 1) for h in (0, 1)])
    start(("core", 0, 0))

    cut_of = {3: 0, 1: 1}
    for h in (0, 1):
        for near in (3, 1):
            arrived(("first", h, near, None))
            start(("first", h, 2, cut_of[near]))
    for f in (3, 1):
        for h in (0, 1):
            start(*[("second", h, f, near, None) for near in (3, 1)])
    forward((7, 0, [("z", 6, 0)]), (1, 3, [("z", 2, 3)]))
    for h in (0, 1):
        arrived(("first", h, 2, 0), ("first", h, 2, 1))
        start(*[("second", h, 2, near, None) for near in (3, 1)])

    def fold(f):
        for h in (0, 1):
            for near in (3, 1):
                arrived(("second", h, f, near, None))
                start(("second", h, f, 2, cut_of[near]))

    fold(0)
    forward((7, 3, [("z", 6, 3)]), (1, 0, [("z", 2, 0)]))
    have(0)
    work(0, 1, [0])
    have(1)
    have(7)
    fold(3)
    forward((6, 0, [("z", 5, 0)]), (2, 3, [("z", 3, 4)]))
    work(0, 1, [1, 7])
    fold(1)
    forward((6, 3, [("z", 5, 2), ("z", 5, 4)]), (2, 0, [("z", 3, 2), ("z", 3, 0)]))
    fold(2)
    work(1, 2, [0, 1, 7])
    have(2)
    have(6)
    work(0, 3, [2, 6])
    forward((5, 0, [("z", 4, 0)]), (3, 4, [("z", 4, 4)]))
    for h in (0, 1):
        for f in range(SIDE):
            arrived(("second", h, f, 2, 0), ("second", h, f, 2, 1))
    work(3, 1, [0, 1, 7, 2, 6])
    forward((5, 2, [("z", 4, 2)]), (3, 2, [("z", 4, 3)]))
    arrived(("core", 5, 0), ("core", 3, 4))
    work(0, 4, [5], (0, 1))
    work(0, 4, [3], (4, 5))
    arrived(("core", 5, 2), ("core", 3, 2))
    work(0, 4, [5, 3], (2, 3))
    forward((5, 4, []), (3, 0, []))
    work(0, 4, [5], (4, 5), (0,))
    work(0, 4, [3], (0, 1), (0,))
    arrived(("core", 5, 4), ("core", 3, 0))
    work(0, 4, [5], (4, 5), (1,))
    work(0, 4, [3], (0, 1), (1,))
    reduce(1)
    start(*[("part", i) for i, (dz, _) in enumerate(others) if dz % 2])
    forward((4, 0, []), (4, 4, []))
    work(0, 4, [4], (0, 1, 4, 5), (0,))
    forward((4, 2, []), (4, 3, []))
    arrived(("core", 4, 0), ("core", 4, 4))
    work(0, 4, [4], (0, 1, 4, 5), (1,))
    work(0, 4, [4], (2, 3), (0,))
    arrived(("core", 4, 2), ("core", 4, 3))
    reduce(0, (2, 3))

    start(*[("part", i) for i, (dz, _) in enumerate(others) if dz % 2 == 0])
    for key, copy in copies.items():
        if key[0] != "part" or others[key[1]][0] % 2:
            copy.wait_send()
    arrived(*[("part", i) for i in range(len(others))])
    out_ref[0:1] = jnp.max(
        jnp.concatenate([part[0, 0:1]] + [inbox[i, 0:1] for i in range(len(others))]), axis=0, keepdims=True
    )
    out_ref[1:2] = jnp.sum(
        jnp.concatenate([part[0, 1:2]] + [inbox[i, 1:2] for i in range(len(others))]), axis=0, keepdims=True
    )
    for i, (dz, _) in enumerate(others):
        if dz % 2 == 0:
            copies["part", i].wait_send()


def on_device(mode_stress, histories):
    n_copies = 18 + 19 + 40 + 15
    out = pl.pallas_call(
        kernel,
        out_shape=jax.ShapeDtypeStruct((2, POINTS), jnp.float32),
        in_specs=[pl.BlockSpec(memory_space=pl.ANY)] * 2,
        out_specs=pl.BlockSpec(memory_space=pltpu.VMEM),
        scratch_shapes=[
            pltpu.VMEM((DEPTH, 2, PARTS, POINTS, SHARE), jnp.bfloat16),
            pltpu.VMEM((SIDE, 2, SIDE, ROWS, 2048), jnp.bfloat16),
            pltpu.VMEM((2, 4 * GROUP, PARTS * POINTS), jnp.float32),
            pltpu.VMEM((2, 2, POINTS), jnp.float32),
            pltpu.VMEM((15, 2, POINTS), jnp.float32),
            pltpu.SemaphoreType.DMA((4,)),
            pltpu.SemaphoreType.DMA((n_copies,)),
            pltpu.SemaphoreType.DMA((n_copies,)),
        ],
        compiler_params=pltpu.CompilerParams(
            collective_id=0, has_side_effects=True, vmem_limit_bytes=(53 * 1024 + 816) * 1024
        ),
        cost_estimate=pl.CostEstimate(
            flops=2 * 1024 * 2048 * 2 * PARTS * POINTS, bytes_accessed=2**20, transcendentals=0
        ),
    )(mode_stress, histories)
    return jnp.sqrt(out[0]), jnp.sqrt(out[1] / STEPS + 1e-06)


def solution(mesh):
    placed = (P(None, "pts", "modes"), P(("pts", "modes"), None))
    return jax.shard_map(
        on_device, mesh=mesh, in_specs=placed, out_specs=(P("pts"), P("pts")), check_vma=False
    )
```

```python
import jax
import jax.numpy as jnp
from jax import lax
from jax.experimental import pallas as pl
from jax.experimental.pallas import tpu as pltpu
from jax.sharding import PartitionSpec as P

STEPS = 16384
MESH = pl.DeviceIdType.MESH
SIDE = 4
DEPTH = 8
PARTS = 6
POINTS = 128
SHARE = 256
ROWS = 32
QUARTER = 16
GROUP = 2 * SIDE * ROWS
PLACE = (0, 1, 3, 2)


def kernel(stress_ref, hist_ref, out_ref, sbuf, hbuf, acc, part, inbox, load_sem, send_sem, recv_sem):
    pts, modes = lax.axis_index("pts"), lax.axis_index("modes")
    x, y = lax.rem(pts // 2, SIDE), pts // (2 * SIDE)
    z, core = (modes // 2) * 2 + lax.rem(pts, 2), lax.rem(modes, 2)

    def device(dx=0, dy=0, dz=0, dc=0):
        px, py = lax.rem(x + dx + SIDE, SIDE), lax.rem(y + dy + SIDE, SIDE)
        pz = lax.rem(z + dz + DEPTH, DEPTH)
        pc = 1 - core if dc else core
        return ((py * SIDE + px) * 2 + lax.rem(pz, 2), (pz // 2) * 2 + pc)

    def along(axis, d):
        return device(dx=d) if axis == 0 else device(dy=d)

    copies = {}

    def remote(key, src, dst, target):
        i = len(copies)
        copies[key] = pltpu.make_async_remote_copy(
            src_ref=src, dst_ref=dst, send_sem=send_sem.at[i], recv_sem=recv_sem.at[i],
            device_id=target, device_id_type=MESH,
        )

    def piece(s, c, low, n):
        return sbuf.at[s, c, pl.ds(low, n)]

    cuts = {s: ((0, 3), (3, 3)) for s in range(DEPTH)}
    cuts[0] = ((0, 6),)
    cuts[3] = cuts[5] = ((0, 2), (2, 2), (4, 2))
    cuts[4] = ((0, 2), (2, 1), (3, 1), (4, 2))
    for sign in (1, -1):
        for step in range(4):
            source, target = (-sign * step) % DEPTH, (-sign * (step + 1)) % DEPTH
            for low, n in cuts[target]:
                if step == 3 and (low < 3) != (sign == 1):
                    continue
                remote(("z", target, low), piece(source, 0, low, n), piece(target, 0, low, n), device(dz=sign))
    for s in range(DEPTH):
        for low, n in cuts[s]:
            remote(("core", s, low), piece(s, 0, low, n), piece(s, 1, low, n), device(dc=1))

    def rows(h, second, first, cut):
        block = hbuf.at[PLACE[second], h, first]
        return block if cut is None else block.at[pl.ds(cut * QUARTER, QUARTER)]

    for h in (0, 1):
        for sign in (1, -1):
            near, cut = (-sign) % SIDE, 0 if sign == 1 else 1
            remote(("first", h, near, None), rows(h, 0, 0, None), rows(h, 0, near, None), along(h, sign))
            remote(("first", h, 2, cut), rows(h, 0, near, cut), rows(h, 0, 2, cut), along(h, sign))
            for f in range(SIDE):
                remote(("second", h, f, near, None), rows(h, 0, f, None), rows(h, near, f, None), along(1 - h, sign))
                remote(("second", h, f, 2, cut), rows(h, near, f, cut), rows(h, 2, f, cut), along(1 - h, sign))

    others = [(dz, dc) for dz in (4, 3, 5, 2, 6, 1, 7, 0) for dc in (0, 1) if (dz, dc) != (0, 0)]
    for i, (dz, dc) in enumerate(others):
        remote(("part", i), part.at[dz % 2], inbox.at[i], device(dz=dz, dc=dc))

    def start(*keys):
        for key in keys:
            copies[key].start()

    def arrived(*keys):
        for key in keys:
            copies[key].wait_recv()

    def product(place, count, s, parts, shares=(0, 1)):
        base = (lax.rem(z + s, DEPTH) // 2) * (2 * SHARE)
        left, right = [], []
        for c in shares:
            first = pl.multiple_of(base + (1 - core if c else core) * SHARE, SHARE)
            left.append(hbuf[place : place + count, :, :, :, pl.ds(first, SHARE)].reshape(count * GROUP, SHARE))
            right.append(jnp.concatenate([sbuf[s, c, i] for i in parts], axis=0))
        left, right = (v[0] if len(v) == 1 else jnp.concatenate(v, axis=1) for v in (left, right))
        return lax.dot_general(left, right, (((1,), (1,)), ((), ())), preferred_element_type=jnp.float32)

    def work(place, count, slots, parts=tuple(range(PARTS)), shares=(0, 1)):
        at = pl.ds(place * GROUP, count * GROUP)
        for s in slots:
            value = product(place, count, s, parts, shares)
            for k, i in enumerate(parts):
                lanes, term = pl.ds(i * POINTS, POINTS), value[:, k * POINTS : (k + 1) * POINTS]
                acc[s % 2, at, lanes] += term

    def work_all(place, count, slot, step, n):
        def one(k, carry):
            s = lax.rem(slot + k * step, DEPTH)
            acc[lax.rem(s, 2), pl.ds(place * GROUP, count * GROUP)] += product(place, count, s, range(PARTS))
            return carry

        lax.fori_loop(0, n, one, 0)

    def clear(k, carry):
        acc[k // 4, pl.ds(pl.multiple_of(lax.rem(k, 4) * GROUP, GROUP), GROUP)] = jnp.zeros(
            (GROUP, PARTS * POINTS), jnp.float32
        )
        return carry

    def squared(s):
        xy, yz, zx = s[0] - s[1], s[1] - s[2], s[2] - s[0]
        return 0.5 * (xy * xy + yz * yz + zx * zx) + 3.0 * (s[3] * s[3] + s[4] * s[4] + s[5] * s[5])

    def reduce(which, last=()):
        highest = jnp.zeros((8, POINTS), jnp.float32)
        summed = jnp.zeros((8, POINTS), jnp.float32)
        for place in range(4):
            value = [acc[which, pl.ds(place * GROUP, GROUP), pl.ds(i * POINTS, POINTS)] for i in range(PARTS)]
            if last:
                rest = product(place, 1, 4, last, (1,))
                for k, i in enumerate(last):
                    value[i] = value[i] + rest[:, k * POINTS : (k + 1) * POINTS]
            square = squared(value).reshape(GROUP // 8, 8, POINTS)
            highest = jnp.maximum(highest, jnp.max(square, axis=0))
            summed = summed + jnp.sum(square, axis=0)
        part[which, 0:1] = jnp.max(highest, axis=0, keepdims=True)
        part[which, 1:2] = jnp.sum(summed, axis=0, keepdims=True)

    barrier = pltpu.get_barrier_semaphore()
    greeted = [device(dz=1), device(dz=-1)] + [along(axis, sign) for axis in (0, 1) for sign in (1, -1)]
    greeted += [device(dc=1)]
    for other in greeted:
        pl.semaphore_signal(barrier, inc=1, device_id=other, device_id_type=MESH)
    loads = [
        pltpu.make_async_copy(stress_ref.at[pl.ds(low, 3)], piece(0, 0, low, 3), load_sem.at[i])
        for i, low in enumerate((0, 3))
    ] + [
        pltpu.make_async_copy(hist_ref.at[pl.ds(h * ROWS, ROWS)], hbuf.at[0, h, 0], load_sem.at[2 + h])
        for h in (0, 1)
    ]
    for load in loads:
        load.start()
    pl.semaphore_wait(barrier, len(greeted))

    def forward(*moves):
        for s, low, onward in moves:
            arrived(("z", s, low))
            start(*onward)
        start(*[("core", s, low) for s, low, _ in moves])

    def have(s):
        arrived(*[("core", s, low) for low, _ in cuts[s]])

    loads[0].wait()
    loads[1].wait()
    start(("z", 7, 0), ("z", 1, 3))
    loads[2].wait()
    loads[3].wait()
    start(*[("first", h, near, None) for near in (3, 1) for h in (0, 1)])
    start(("z", 7, 3), ("z", 1, 0))
    start(*[("second", h, 0, near, None) for near in (3, 1) for h in (0, 1)])
    start(("core", 0, 0))
    lax.fori_loop(0, 8, clear, 0)

    cut_of = {3: 0, 1: 1}
    for h in (0, 1):
        for near in (3, 1):
            arrived(("first", h, near, None))
            start(("first", h, 2, cut_of[near]))
    for f in (3, 1):
        for h in (0, 1):
            start(*[("second", h, f, near, None) for near in (3, 1)])
    forward((7, 0, [("z", 6, 0)]), (1, 3, [("z", 2, 3)]))
    for h in (0, 1):
        arrived(("first", h, 2, 0), ("first", h, 2, 1))
        start(*[("second", h, 2, near, None) for near in (3, 1)])

    def fold(f):
        for h in (0, 1):
            for near in (3, 1):
                arrived(("second", h, f, near, None))
                start(("second", h, f, 2, cut_of[near]))

    fold(0)
    forward((7, 3, [("z", 6, 3)]), (1, 0, [("z", 2, 0)]))
    have(0)
    have(1)
    have(7)
    fold(3)
    forward((6, 0, [("z", 5, 0)]), (2, 3, [("z", 3, 4)]))
    work_all(0, 1, 7, 1, 3)
    fold(1)
    forward((6, 3, [("z", 5, 2), ("z", 5, 4)]), (2, 0, [("z", 3, 2), ("z", 3, 0)]))
    fold(2)
    work_all(1, 2, 7, 1, 3)
    have(2)
    have(6)
    work_all(0, 3, 2, 4, 2)
    forward((5, 0, [("z", 4, 0)]), (3, 4, [("z", 4, 4)]))
    for h in (0, 1):
        for f in range(SIDE):
            arrived(("second", h, f, 2, 0), ("second", h, f, 2, 1))
    work_all(3, 1, 7, 1, 3)
    forward((5, 2, [("z", 4, 2)]), (3, 2, [("z", 4, 3)]))
    work_all(3, 1, 2, 4, 2)
    arrived(("core", 5, 0), ("core", 3, 4))
    work(0, 4, [5], (0, 1))
    work(0, 4, [3], (4, 5))
    arrived(("core", 5, 2), ("core", 3, 2))
    work(0, 4, [5, 3], (2, 3))
    forward((5, 4, []), (3, 0, []))
    work(0, 4, [5], (4, 5), (0,))
    work(0, 4, [3], (0, 1), (0,))
    arrived(("core", 5, 4), ("core", 3, 0))
    work(0, 4, [5], (4, 5), (1,))
    work(0, 4, [3], (0, 1), (1,))
    reduce(1)
    start(*[("part", i) for i, (dz, _) in enumerate(others) if dz % 2])
    forward((4, 0, []), (4, 4, []))
    work(0, 4, [4], (0, 1, 4, 5), (0,))
    forward((4, 2, []), (4, 3, []))
    arrived(("core", 4, 0), ("core", 4, 4))
    work(0, 4, [4], (0, 1, 4, 5), (1,))
    work(0, 4, [4], (2, 3), (0,))
    arrived(("core", 4, 2), ("core", 4, 3))
    reduce(0, (2, 3))

    start(*[("part", i) for i, (dz, _) in enumerate(others) if dz % 2 == 0])
    for key, copy in copies.items():
        if key[0] != "part" or others[key[1]][0] % 2:
            copy.wait_send()
    arrived(*[("part", i) for i in range(len(others))])
    out_ref[0:1] = jnp.max(
        jnp.concatenate([part[0, 0:1]] + [inbox[i, 0:1] for i in range(len(others))]), axis=0, keepdims=True
    )
    out_ref[1:2] = jnp.sum(
        jnp.concatenate([part[0, 1:2]] + [inbox[i, 1:2] for i in range(len(others))]), axis=0, keepdims=True
    )
    for i, (dz, _) in enumerate(others):
        if dz % 2 == 0:
            copies["part", i].wait_send()


def on_device(mode_stress, histories):
    n_copies = 18 + 19 + 40 + 15
    out = pl.pallas_call(
        kernel,
        out_shape=jax.ShapeDtypeStruct((2, POINTS), jnp.float32),
        in_specs=[pl.BlockSpec(memory_space=pl.ANY)] * 2,
        out_specs=pl.BlockSpec(memory_space=pltpu.VMEM),
        scratch_shapes=[
            pltpu.VMEM((DEPTH, 2, PARTS, POINTS, SHARE), jnp.bfloat16),
            pltpu.VMEM((SIDE, 2, SIDE, ROWS, 2048), jnp.bfloat16),
            pltpu.VMEM((2, 4 * GROUP, PARTS * POINTS), jnp.float32),
            pltpu.VMEM((2, 2, POINTS), jnp.float32),
            pltpu.VMEM((15, 2, POINTS), jnp.float32),
            pltpu.SemaphoreType.DMA((4,)),
            pltpu.SemaphoreType.DMA((n_copies,)),
            pltpu.SemaphoreType.DMA((n_copies,)),
        ],
        compiler_params=pltpu.CompilerParams(
            collective_id=0, has_side_effects=True, vmem_limit_bytes=(53 * 1024 + 816) * 1024
        ),
        cost_estimate=pl.CostEstimate(
            flops=2 * 1024 * 2048 * 2 * PARTS * POINTS, bytes_accessed=2**20, transcendentals=0
        ),
    )(mode_stress, histories)
    return jnp.sqrt(out[0]), jnp.sqrt(out[1] / STEPS + 1e-06)


def solution(mesh):
    placed = (P(None, "pts", "modes"), P(("pts", "modes"), None))
    return jax.shard_map(
        on_device, mesh=mesh, in_specs=placed, out_specs=(P("pts"), P("pts")), check_vma=False
    )
```

```python
import jax
import jax.numpy as jnp
from jax import lax
from jax.experimental import pallas as pl
from jax.experimental.pallas import tpu as pltpu
from jax.sharding import PartitionSpec as P

STEPS = 16384
MESH = pl.DeviceIdType.MESH
SIDE = 4
DEPTH = 8
PARTS = 6
POINTS = 128
SHARE = 256
ROWS = 32
QUARTER = 16
GROUP = 2 * SIDE * ROWS
PLACE = (0, 1, 3, 2)


def kernel(stress_ref, hist_ref, out_ref, sbuf, hbuf, acc, part, inbox, load_sem, send_sem, recv_sem):
    pts, modes = lax.axis_index("pts"), lax.axis_index("modes")
    x, y = lax.rem(pts // 2, SIDE), pts // (2 * SIDE)
    z, core = (modes // 2) * 2 + lax.rem(pts, 2), lax.rem(modes, 2)

    def device(dx=0, dy=0, dz=0, dc=0):
        px, py = lax.rem(x + dx + SIDE, SIDE), lax.rem(y + dy + SIDE, SIDE)
        pz = lax.rem(z + dz + DEPTH, DEPTH)
        pc = 1 - core if dc else core
        return ((py * SIDE + px) * 2 + lax.rem(pz, 2), (pz // 2) * 2 + pc)

    def along(axis, d):
        return device(dx=d) if axis == 0 else device(dy=d)

    copies = {}

    def remote(key, src, dst, target):
        i = len(copies)
        copies[key] = pltpu.make_async_remote_copy(
            src_ref=src, dst_ref=dst, send_sem=send_sem.at[i], recv_sem=recv_sem.at[i],
            device_id=target, device_id_type=MESH,
        )

    def piece(s, c, low, n):
        return sbuf.at[s, c, pl.ds(low, n)]

    cuts = {s: ((0, 3), (3, 3)) for s in range(DEPTH)}
    cuts[0] = ((0, 6),)
    cuts[3] = cuts[5] = ((0, 2), (2, 2), (4, 2))
    cuts[4] = ((0, 2), (2, 1), (3, 1), (4, 2))
    for sign in (1, -1):
        for step in range(4):
            source, target = (-sign * step) % DEPTH, (-sign * (step + 1)) % DEPTH
            for low, n in cuts[target]:
                if step == 3 and (low < 3) != (sign == 1):
                    continue
                remote(("z", target, low), piece(source, 0, low, n), piece(target, 0, low, n), device(dz=sign))
    for s in range(DEPTH):
        for low, n in cuts[s]:
            remote(("core", s, low), piece(s, 0, low, n), piece(s, 1, low, n), device(dc=1))

    def rows(h, second, first, cut):
        block = hbuf.at[PLACE[second], h, first]
        return block if cut is None else block.at[pl.ds(cut * QUARTER, QUARTER)]

    for h in (0, 1):
        for sign in (1, -1):
            near, cut = (-sign) % SIDE, 0 if sign == 1 else 1
            remote(("first", h, near, None), rows(h, 0, 0, None), rows(h, 0, near, None), along(h, sign))
            remote(("first", h, 2, cut), rows(h, 0, near, cut), rows(h, 0, 2, cut), along(h, sign))
            for f in range(SIDE):
                remote(("second", h, f, near, None), rows(h, 0, f, None), rows(h, near, f, None), along(1 - h, sign))
                remote(("second", h, f, 2, cut), rows(h, near, f, cut), rows(h, 2, f, cut), along(1 - h, sign))

    others = [(dz, dc) for dz in (4, 3, 5, 2, 6, 1, 7, 0) for dc in (0, 1) if (dz, dc) != (0, 0)]
    for i, (dz, dc) in enumerate(others):
        remote(("part", i), part.at[dz % 2], inbox.at[i], device(dz=dz, dc=dc))

    def start(*keys):
        for key in keys:
            copies[key].start()

    def arrived(*keys):
        for key in keys:
            copies[key].wait_recv()

    def product(place, count, s, parts, shares=(0, 1)):
        base = (lax.rem(z + s, DEPTH) // 2) * (2 * SHARE)
        left, right = [], []
        for c in shares:
            first = pl.multiple_of(base + (1 - core if c else core) * SHARE, SHARE)
            left.append(hbuf[place : place + count, :, :, :, pl.ds(first, SHARE)].reshape(count * GROUP, SHARE))
            right.append(jnp.concatenate([sbuf[s, c, i] for i in parts], axis=0))
        left, right = (v[0] if len(v) == 1 else jnp.concatenate(v, axis=1) for v in (left, right))
        return lax.dot_general(left, right, (((1,), (1,)), ((), ())), preferred_element_type=jnp.float32)

    def work(place, count, slots, parts=tuple(range(PARTS)), shares=(0, 1)):
        at = pl.ds(place * GROUP, count * GROUP)
        for s in slots:
            value = product(place, count, s, parts, shares)
            for k, i in enumerate(parts):
                lanes, term = pl.ds(i * POINTS, POINTS), value[:, k * POINTS : (k + 1) * POINTS]
                acc[s % 2, at, lanes] += term

    def work_all(place, count, slot, step, n):
        def one(k, carry):
            s = lax.rem(slot + k * step, DEPTH)
            acc[lax.rem(s, 2), pl.ds(place * GROUP, count * GROUP)] += product(place, count, s, range(PARTS))
            return carry

        lax.fori_loop(0, n, one, 0)

    def clear(k, carry):
        acc[k // 4, pl.ds(pl.multiple_of(lax.rem(k, 4) * GROUP, GROUP), GROUP)] = jnp.zeros(
            (GROUP, PARTS * POINTS), jnp.float32
        )
        return carry

    def squared(s):
        xy, yz, zx = s[0] - s[1], s[1] - s[2], s[2] - s[0]
        return 0.5 * (xy * xy + yz * yz + zx * zx) + 3.0 * (s[3] * s[3] + s[4] * s[4] + s[5] * s[5])

    def reduce(which, last=()):
        highest = jnp.zeros((8, POINTS), jnp.float32)
        summed = jnp.zeros((8, POINTS), jnp.float32)
        for place in range(4):
            value = [acc[which, pl.ds(place * GROUP, GROUP), pl.ds(i * POINTS, POINTS)] for i in range(PARTS)]
            if last:
                rest = product(place, 1, 4, last, (1,))
                for k, i in enumerate(last):
                    value[i] = value[i] + rest[:, k * POINTS : (k + 1) * POINTS]
            square = squared(value).reshape(GROUP // 8, 8, POINTS)
            highest = jnp.maximum(highest, jnp.max(square, axis=0))
            summed = summed + jnp.sum(square, axis=0)
        part[which, 0:1] = jnp.max(highest, axis=0, keepdims=True)
        part[which, 1:2] = jnp.sum(summed, axis=0, keepdims=True)

    barrier = pltpu.get_barrier_semaphore()
    greeted = [device(dz=1), device(dz=-1)] + [along(axis, sign) for axis in (0, 1) for sign in (1, -1)]
    greeted += [device(dc=1)]
    for other in greeted:
        pl.semaphore_signal(barrier, inc=1, device_id=other, device_id_type=MESH)
    loads = [
        pltpu.make_async_copy(stress_ref.at[pl.ds(low, 3)], piece(0, 0, low, 3), load_sem.at[i])
        for i, low in enumerate((0, 3))
    ] + [
        pltpu.make_async_copy(hist_ref.at[pl.ds(h * ROWS, ROWS)], hbuf.at[0, h, 0], load_sem.at[2 + h])
        for h in (0, 1)
    ]
    for load in loads:
        load.start()
    pl.semaphore_wait(barrier, len(greeted))

    def forward(*moves):
        for s, low, onward in moves:
            arrived(("z", s, low))
            start(*onward, ("core", s, low))

    def have(s):
        arrived(*[("core", s, low) for low, _ in cuts[s]])

    loads[0].wait()
    loads[1].wait()
    start(("z", 7, 0), ("z", 1, 3))
    loads[2].wait()
    loads[3].wait()
    start(*[("first", h, near, None) for near in (3, 1) for h in (0, 1)])
    start(("z", 7, 3), ("z", 1, 0))
    start(*[("second", h, 0, near, None) for near in (3, 1) for h in (0, 1)])
    start(("core", 0, 0))
    lax.fori_loop(0, 8, clear, 0)

    cut_of = {3: 0, 1: 1}
    for h in (0, 1):
        for near in (3, 1):
            arrived(("first", h, near, None))
            start(("first", h, 2, cut_of[near]))
    for f in (3, 1):
        for h in (0, 1):
            start(*[("second", h, f, near, None) for near in (3, 1)])
    forward((7, 0, [("z", 6, 0)]), (1, 3, [("z", 2, 3)]))
    for h in (0, 1):
        arrived(("first", h, 2, 0), ("first", h, 2, 1))
        start(*[("second", h, 2, near, None) for near in (3, 1)])

    def fold(f):
        for h in (0, 1):
            for near in (3, 1):
                arrived(("second", h, f, near, None))
                start(("second", h, f, 2, cut_of[near]))

    fold(0)
    forward((7, 3, [("z", 6, 3)]), (1, 0, [("z", 2, 0)]))
    have(0)
    have(1)
    have(7)
    fold(3)
    forward((6, 0, [("z", 5, 0)]), (2, 3, [("z", 3, 4)]))
    work_all(0, 1, 7, 1, 3)
    fold(1)
    forward((6, 3, [("z", 5, 2), ("z", 5, 4)]), (2, 0, [("z", 3, 2), ("z", 3, 0)]))
    fold(2)
    work_all(1, 2, 7, 1, 3)
    have(2)
    have(6)
    work_all(0, 3, 2, 4, 2)
    forward((5, 0, [("z", 4, 0)]), (3, 4, [("z", 4, 4)]))
    for h in (0, 1):
        for f in range(SIDE):
            arrived(("second", h, f, 2, 0), ("second", h, f, 2, 1))
    work_all(3, 1, 6, 1, 5)
    forward((5, 2, [("z", 4, 2)]), (3, 2, [("z", 4, 3)]))
    arrived(("core", 5, 0), ("core", 3, 4))
    work(0, 4, [5], (0, 1))
    work(0, 4, [3], (4, 5))
    arrived(("core", 5, 2), ("core", 3, 2))
    work(0, 4, [5, 3], (2, 3))
    forward((5, 4, []), (3, 0, []))
    work(0, 4, [5], (4, 5), (0,))
    work(0, 4, [3], (0, 1), (0,))
    arrived(("core", 5, 4), ("core", 3, 0))
    work(0, 4, [5], (4, 5), (1,))
    work(0, 4, [3], (0, 1), (1,))
    forward((4, 0, []), (4, 4, []))
    reduce(1)
    start(*[("part", i) for i, (dz, _) in enumerate(others) if dz % 2])
    work(0, 4, [4], (0, 1, 4, 5), (0,))
    forward((4, 2, []), (4, 3, []))
    arrived(("core", 4, 0), ("core", 4, 4))
    work(0, 4, [4], (0, 1, 4, 5), (1,))
    work(0, 4, [4], (2, 3), (0,))
    arrived(("core", 4, 2), ("core", 4, 3))
    reduce(0, (2, 3))

    start(*[("part", i) for i, (dz, _) in enumerate(others) if dz % 2 == 0])
    for key, copy in copies.items():
        if key[0] != "part" or others[key[1]][0] % 2:
            copy.wait_send()
    arrived(*[("part", i) for i in range(len(others))])
    out_ref[0:1] = jnp.max(
        jnp.concatenate([part[0, 0:1]] + [inbox[i, 0:1] for i in range(len(others))]), axis=0, keepdims=True
    )
    out_ref[1:2] = jnp.sum(
        jnp.concatenate([part[0, 1:2]] + [inbox[i, 1:2] for i in range(len(others))]), axis=0, keepdims=True
    )
    for i, (dz, _) in enumerate(others):
        if dz % 2 == 0:
            copies["part", i].wait_send()


def on_device(mode_stress, histories):
    n_copies = 18 + 19 + 40 + 15
    out = pl.pallas_call(
        kernel,
        out_shape=jax.ShapeDtypeStruct((2, POINTS), jnp.float32),
        in_specs=[pl.BlockSpec(memory_space=pl.ANY)] * 2,
        out_specs=pl.BlockSpec(memory_space=pltpu.VMEM),
        scratch_shapes=[
            pltpu.VMEM((DEPTH, 2, PARTS, POINTS, SHARE), jnp.bfloat16),
            pltpu.VMEM((SIDE, 2, SIDE, ROWS, 2048), jnp.bfloat16),
            pltpu.VMEM((2, 4 * GROUP, PARTS * POINTS), jnp.float32),
            pltpu.VMEM((2, 2, POINTS), jnp.float32),
            pltpu.VMEM((15, 2, POINTS), jnp.float32),
            pltpu.SemaphoreType.DMA((4,)),
            pltpu.SemaphoreType.DMA((n_copies,)),
            pltpu.SemaphoreType.DMA((n_copies,)),
        ],
        compiler_params=pltpu.CompilerParams(
            collective_id=0, has_side_effects=True, vmem_limit_bytes=(53 * 1024 + 816) * 1024
        ),
        cost_estimate=pl.CostEstimate(
            flops=2 * 1024 * 2048 * 2 * PARTS * POINTS, bytes_accessed=2**20, transcendentals=0
        ),
    )(mode_stress, histories)
    return jnp.sqrt(out[0]), jnp.sqrt(out[1] / STEPS + 1e-06)


def solution(mesh):
    placed = (P(None, "pts", "modes"), P(("pts", "modes"), None))
    return jax.shard_map(
        on_device, mesh=mesh, in_specs=placed, out_specs=(P("pts"), P("pts")), check_vma=False
    )
```
